32 devices in a mesh: wide: 32 (over z, y, x, core), narrow: 1.
Axes of the slice: x: 2, y: 2, z: 4, core: 2. Of those that a mesh axis runs over, the one named last changes fastest.
Arguments:
- field: float32 [256, 44, 512], P('wide', 'narrow')
- sketch_one: float32 [512, 128], replicated, may hold values from -6 to 6
- sketch_two: float32 [256, 128], replicated, may hold values from -6 to 6
- ranks: int32 [2], replicated, may hold values from 64 to 128, as said below
Outputs:
- core: float32 [128, 44, 128], P('wide', 'narrow')
The draws below stay inside these ranges and needn't reach their ends.
Inputs may be any that keep to these rules, and one draw needn't show every extreme that they name: One of the two ranks equals 128.
All inputs are finite; a program needn't handle non-finite values.
Results may differ from the reference program's by a relative error of at most 0.00022.
Values sent between devices are 32-bit elements; how exact they have to be, the bound alone decides.
A program may use at most 64 MiB of HBM per device.

```python
import math
import jax
import jax.numpy as jnp
from jax import lax

N1 = 512
Y_DEV = 8
Z_DEV = 4
C = 11
RMAX = 128
N2 = 256
N3 = 4


def draw_field(key, part):
    keys = jax.random.split(jax.random.fold_in(key, 11), 6)
    total = N3 * C
    spread = 3.0
    mixing = 0.6
    base = jax.random.normal(keys[2], (N1, N2, total), jnp.float32)
    first = jax.random.normal(keys[3], (N1 // 4, 1, N2, total), jnp.float32)
    second = jax.random.normal(keys[4], (N1, N2 // 4, 1, total), jnp.float32)
    row_scale = jnp.exp(jax.random.uniform(keys[0], (N1, 1, 1), jnp.float32) * math.log(spread))
    col_scale = jnp.exp(jax.random.uniform(keys[1], (1, N2, 1), jnp.float32) * math.log(spread))
    mixed = (base.reshape(N1 // 4, 4, N2, total) + mixing * first).reshape(N1, N2, total)
    mixed = (mixed.reshape(N1, N2 // 4, 4, total) + mixing * second).reshape(N1, N2, total)
    scaled = row_scale * col_scale * mixed / math.sqrt(1.0 + 2.0 * mixing * mixing)
    narrow_count = N3 // Z_DEV
    owners = N2 // Y_DEV * narrow_count
    joint = (jnp.arange(N2) // Y_DEV)[:, None] * narrow_count + (jnp.arange(total) // (Z_DEV * C))[None, :]
    paired = jax.random.permutation(keys[5], N1)
    owned = paired[joint % N1]
    heavy = jnp.arange(N1)[:, None, None] == owned[None, :, :]
    boost = math.sqrt(2.0 * owners)
    scaled = jnp.where(heavy, boost * scaled, scaled)
    return jnp.transpose(scaled, (1, 2, 0)).astype(jnp.float32)


def draw_ranks(key, part):
    keys = jax.random.split(jax.random.fold_in(key, 23), 2)
    which = jax.random.randint(keys[0], (), 0, 2)
    other = jax.random.randint(keys[1], (), RMAX // 2, RMAX + 1)
    return jnp.where(jnp.arange(2) == which, RMAX, other).astype(jnp.int32)


def gaussian(own_key, extent, deviation, most, held_as=jnp.bfloat16):
    return jnp.clip(deviation * jax.random.normal(own_key, extent, jnp.float32), -most, most).astype(held_as)


def setup_inputs(seed: int = 0) -> dict:
    seeds = jax.random.split(jax.random.key(seed), 5)
    return {
        "field": draw_field(jax.random.fold_in(seeds[4], 71), 0),
        "sketch_one": gaussian(seeds[1], (N1, RMAX), 1.0, 6.0, jnp.float32),
        "sketch_two": gaussian(seeds[2], (N2, RMAX), 1.0, 6.0, jnp.float32),
        "ranks": draw_ranks(jax.random.fold_in(seeds[4], 71), 0),
    }


def make_basis(gram, sketch, rank):
    keep = (jnp.arange(sketch.shape[1]) < rank).astype(jnp.float32)
    sketched = jnp.dot(gram, sketch * keep, precision=lax.Precision.HIGHEST)
    inner = jnp.dot(sketched.T, sketched, precision=lax.Precision.HIGHEST) + jnp.diag(1.0 - keep)
    lower = jnp.linalg.cholesky(inner)
    return jax.scipy.linalg.solve_triangular(lower, sketched.T, lower=True)

def reference(field, sketch_one, sketch_two, ranks):
    highest = lax.Precision.HIGHEST
    gram_one = jnp.einsum('ykn,ykm->nm', field, field, precision=highest)
    basis_one = make_basis(gram_one, sketch_one, ranks[0])
    core_one = jnp.einsum('rn,ykn->rky', basis_one, field, precision=highest)
    gram_two = jnp.einsum('rkn,rkm->nm', core_one, core_one, precision=highest)
    basis_two = make_basis(gram_two, sketch_two, ranks[1])
    return jnp.einsum('sn,rkn->rks', basis_two, core_one, precision=highest)
```

```python
import functools

import jax
import jax.numpy as jnp
from jax import lax
from jax.experimental import pallas as pl
from jax.experimental.pallas import tpu as pltpu
from jax.sharding import PartitionSpec as P

HIGHEST = lax.Precision.HIGHEST
MESH = pl.DeviceIdType.MESH


def make_basis(local, sketch, rank):
    keep = (jnp.arange(sketch.shape[1]) < rank).astype(jnp.float32)
    masked = sketch * keep
    part = jnp.einsum("akn,ns->aks", local, masked, precision=HIGHEST)
    part = jnp.einsum("akn,aks->ns", local, part, precision=HIGHEST)
    sketched = lax.psum(part, ("wide", "narrow"))
    inner = jnp.dot(sketched.T, sketched, precision=HIGHEST) + jnp.diag(1.0 - keep)
    lower = jnp.linalg.cholesky(inner)
    return jax.scipy.linalg.solve_triangular(lower, sketched.T, lower=True)


def general(field, sketch_one, sketch_two, ranks):
    basis_one = make_basis(field, sketch_one, ranks[0])
    core_one = jnp.einsum("rn,ykn->rky", basis_one, field, precision=HIGHEST)
    regrouped = lax.all_to_all(core_one, "wide", split_axis=0, concat_axis=2, tiled=True)
    basis_two = make_basis(regrouped, sketch_two, ranks[1])
    return jnp.einsum("sn,rkn->rks", basis_two, regrouped, precision=HIGHEST)


def dot(a, b, dims):
    return lax.dot_general(
        a, b, (dims, ((), ())), precision=HIGHEST, preferred_element_type=jnp.float32
    )


NN = ((1,), (0,))
NT = ((1,), (1,))
TN = ((0,), (0,))
BLOCK = 8


def inverse_factor(work, linv):
    size = linv.shape[0]
    tile = (BLOCK, size)
    sub = lax.broadcasted_iota(jnp.int32, tile, 0)

    def body(i, carry):
        r0 = pl.multiple_of(i * BLOCK, BLOCK)
        rows_a = work[pl.ds(r0, BLOCK), :size]
        rows_t = work[pl.ds(r0, BLOCK), size:]
        rolled = pltpu.roll(rows_a, lax.rem(size - r0, size), 1)
        d = {}
        for q in range(BLOCK):
            column = jnp.broadcast_to(rolled[:, q : q + 1], tile)
            for p in range(q, BLOCK):
                d[p, q] = jnp.broadcast_to(column[p : p + 1, :], tile)
        done_a, done_t = [], []
        panel_a = jnp.zeros(tile, jnp.float32)
        panel_t = jnp.zeros(tile, jnp.float32)
        for j in range(BLOCK):
            x = d[j, j]
            y = lax.rsqrt(x)
            y = y * (1.5 - 0.5 * ((x * y) * y))
            for p in range(j + 1, BLOCK):
                d[p, j] = d[p, j] * y
            for q in range(j + 1, BLOCK):
                for p in range(q, BLOCK):
                    d[p, q] = d[p, q] - d[p, j] * d[q, j]
            ra = jnp.broadcast_to(rows_a[j : j + 1, :], tile)
            rt = jnp.broadcast_to(rows_t[j : j + 1, :], tile)
            for k in range(j):
                ra = ra - d[j, k] * done_a[k]
                rt = rt - d[j, k] * done_t[k]
            ra = ra * y
            rt = rt * y
            done_a.append(ra)
            done_t.append(rt)
            panel_a = jnp.where(sub == j, ra, panel_a)
            panel_t = jnp.where(sub == j, rt, panel_t)
        linv[pl.ds(r0, BLOCK), :] = panel_t
        both = jnp.concatenate([panel_a, panel_t], axis=1)
        work[...] = work[...] - dot(panel_a, both, TN)
        return carry

    lax.fori_loop(0, size // BLOCK, body, 0)


def fill_work(work, inner, keep_row, size):
    row = lax.broadcasted_iota(jnp.int32, (size, size), 0)
    col = lax.broadcasted_iota(jnp.int32, (size, size), 1)
    eye = (row == col).astype(jnp.float32)
    work[:, :size] = inner + eye * (1.0 - keep_row)
    work[:, size:] = eye


def kernel(
    n, field, sketch_one, sketch_two, ranks, out,
    flat, part_one, got_one, full_one, work, linv, core, give, have,
    part_two, got_two, full_two, send_sem, recv_sem,
):
    me = lax.axis_index("wide")
    ydev, kdim, n1 = field.shape
    size = sketch_one.shape[1]
    n2 = sketch_two.shape[0]
    stride = flat.shape[0] // ydev
    per = size // n
    c1 = n1 // n
    c2 = n2 // n

    barrier = pltpu.get_barrier_semaphore()

    def greet(i, carry):
        peer = lax.rem(me + 1 + i, n)
        pl.semaphore_signal(barrier, inc=1, device_id={"wide": peer}, device_id_type=MESH)
        return carry

    lax.fori_loop(0, n - 1, greet, 0)

    def exchange(phase, source, target, whole):
        def start(i, carry):
            peer = lax.rem(me + 1 + i, n)
            pltpu.make_async_remote_copy(
                src_ref=source(peer), dst_ref=target(i),
                send_sem=send_sem.at[phase], recv_sem=recv_sem.at[phase],
                device_id={"wide": peer}, device_id_type=MESH,
            ).start()
            return carry

        lax.fori_loop(0, n - 1, start, 0)
        everything = pltpu.make_async_remote_copy(
            src_ref=whole, dst_ref=whole,
            send_sem=send_sem.at[phase], recv_sem=recv_sem.at[phase],
            device_id={"wide": lax.rem(me + 1, n)}, device_id_type=MESH,
        )
        everything.wait_recv()
        everything.wait_send()

    lane = lax.broadcasted_iota(jnp.int32, (1, size), 1)
    keep_one = (lane < ranks[0]).astype(jnp.float32)
    keep_two = (lane < ranks[1]).astype(jnp.float32)

    for y in range(ydev):
        flat[y * stride : y * stride + kdim, :] = field[y]
        flat[y * stride + kdim : (y + 1) * stride, :] = jnp.zeros(
            (stride - kdim, n1), jnp.float32
        )
    projected = dot(flat[...], sketch_one[...] * keep_one, NN)
    part_one[...] = dot(projected, flat[...], TN).T
    masked_two = (sketch_two[...] * keep_two).T

    pl.semaphore_wait(barrier, n - 1)

    exchange(
        0,
        lambda p: part_one.at[pl.ds(pl.multiple_of(p * c1, c1), c1), :],
        lambda i: got_one.at[i],
        got_one,
    )
    mine_one = pl.ds(pl.multiple_of(me * c1, c1), c1)
    full_one[mine_one, :] = jnp.sum(got_one[...], axis=0) + part_one[mine_one, :]
    exchange(
        1,
        lambda p: full_one.at[mine_one, :],
        lambda i: full_one.at[mine_one, :],
        full_one.at[pl.ds(0, n1 - c1), :],
    )
    sk = full_one[...]
    fill_work(work, dot(sk, sk, TN), keep_one, size)
    rotated = dot(flat[...], sk, NN)
    inverse_factor(work, linv)
    mixed = dot(linv[...], rotated, NT)
    for t in range(ydev // 2):
        core[t] = mixed[:, 2 * stride * t : 2 * stride * (t + 1)]

    low = lax.broadcasted_iota(jnp.int32, (n, 2 * stride), 1) < stride
    for half in range(per // 2):
        for t in range(ydev // 2):
            first = core[t, pl.ds(2 * half, n, stride=per), :]
            second = core[t, pl.ds(2 * half + 1, n, stride=per), :]
            even = jnp.where(low, first, pltpu.roll(second, stride, 1))
            odd = jnp.where(low, pltpu.roll(first, stride, 1), second)
            give[half, pl.ds(2 * t, n, stride=ydev), :] = even
            give[half, pl.ds(2 * t + 1, n, stride=ydev), :] = odd
    mine_y = pl.ds(pl.multiple_of(me * ydev, ydev), ydev)
    have[:, mine_y, :] = give[:, mine_y, :]
    exchange(
        2,
        lambda p: give.at[:, pl.ds(pl.multiple_of(p * ydev, ydev), ydev), :],
        lambda i: have.at[:, mine_y, :],
        have.at[:, pl.ds(0, n2 - ydev), :],
    )

    total = jnp.zeros((n2, size), jnp.float32)
    for half in range(per // 2):
        fibers = have[half]
        total = total + dot(fibers, dot(masked_two, fibers, NN), NT)
    part_two[...] = total
    exchange(
        3,
        lambda p: part_two.at[pl.ds(pl.multiple_of(p * c2, c2), c2), :],
        lambda i: got_two.at[i],
        got_two,
    )
    mine_two = pl.ds(pl.multiple_of(me * c2, c2), c2)
    full_two[mine_two, :] = jnp.sum(got_two[...], axis=0) + part_two[mine_two, :]
    exchange(
        4,
        lambda p: full_two.at[mine_two, :],
        lambda i: full_two.at[mine_two, :],
        full_two.at[pl.ds(0, n2 - c2), :],
    )
    sk = full_two[...]
    fill_work(work, dot(sk, sk, TN), keep_two, size)
    spun = [dot(have[half], sk, TN) for half in range(per // 2)]
    inverse_factor(work, linv)
    for half in range(per // 2):
        done = dot(spun[half], linv[...], NT)
        for i in range(2):
            out[2 * half + i] = done[stride * i : stride * i + kdim, :]


def fused(n, field, sketch_one, sketch_two, ranks):
    ydev, kdim, n1 = field.shape
    n2, size = sketch_two.shape
    stride = size // 2
    vmem = pl.BlockSpec(memory_space=pltpu.VMEM)
    f32 = jnp.float32
    return pl.pallas_call(
        functools.partial(kernel, n),
        out_shape=jax.ShapeDtypeStruct((size // n, kdim, size), f32),
        in_specs=[vmem, vmem, vmem, pl.BlockSpec(memory_space=pltpu.SMEM)],
        out_specs=vmem,
        scratch_shapes=[
            pltpu.VMEM((ydev * stride, n1), f32),
            pltpu.VMEM((n1, size), f32),
            pltpu.VMEM((n - 1, n1 // n, size), f32),
            pltpu.VMEM((n1, size), f32),
            pltpu.VMEM((size, 2 * size), f32),
            pltpu.VMEM((size, size), f32),
            pltpu.VMEM((ydev // 2, size, 2 * stride), f32),
            pltpu.VMEM((size // n // 2, n2, size), f32),
            pltpu.VMEM((size // n // 2, n2, size), f32),
            pltpu.VMEM((n2, size), f32),
            pltpu.VMEM((n - 1, n2 // n, size), f32),
            pltpu.VMEM((n2, size), f32),
            pltpu.SemaphoreType.DMA((5,)),
            pltpu.SemaphoreType.DMA((5,)),
        ],
        compiler_params=pltpu.CompilerParams(
            collective_id=0, has_side_effects=True, vmem_limit_bytes=32 * 1024 * 1024
        ),
        cost_estimate=pl.CostEstimate(
            flops=600_000_000, bytes_accessed=2_000_000, transcendentals=256
        ),
    )(field, sketch_one, sketch_two, ranks)


def solution(mesh):
    n = mesh.shape["wide"]

    def per_device(field, sketch_one, sketch_two, ranks):
        ydev, kdim, n1 = field.shape
        n2, size = sketch_two.shape
        fits = (
            mesh.shape["narrow"] == 1
            and size == 128
            and ydev == 8
            and kdim <= size // 2
            and size % (2 * n) == 0
            and n1 % (8 * n) == 0
            and n2 == 8 * n
        )
        if fits:
            return fused(n, field, sketch_one, sketch_two, ranks)
        return general(field, sketch_one, sketch_two, ranks)

    return jax.shard_map(
        per_device,
        mesh=mesh,
        in_specs=(P("wide", "narrow", None), P(), P(), P()),
        out_specs=P("wide", "narrow", None),
        check_vma=False,
    )
```

```python
import functools

import jax
import jax.numpy as jnp
from jax import lax
from jax.experimental import pallas as pl
from jax.experimental.pallas import tpu as pltpu
from jax.sharding import PartitionSpec as P

HIGHEST = lax.Precision.HIGHEST
MESH = pl.DeviceIdType.MESH


def make_basis(local, sketch, rank):
    keep = (jnp.arange(sketch.shape[1]) < rank).astype(jnp.float32)
    masked = sketch * keep
    part = jnp.einsum("akn,ns->aks", local, masked, precision=HIGHEST)
    part = jnp.einsum("akn,aks->ns", local, part, precision=HIGHEST)
    sketched = lax.psum(part, ("wide", "narrow"))
    inner = jnp.dot(sketched.T, sketched, precision=HIGHEST) + jnp.diag(1.0 - keep)
    lower = jnp.linalg.cholesky(inner)
    return jax.scipy.linalg.solve_triangular(lower, sketched.T, lower=True)


def general(field, sketch_one, sketch_two, ranks):
    basis_one = make_basis(field, sketch_one, ranks[0])
    core_one = jnp.einsum("rn,ykn->rky", basis_one, field, precision=HIGHEST)
    regrouped = lax.all_to_all(core_one, "wide", split_axis=0, concat_axis=2, tiled=True)
    basis_two = make_basis(regrouped, sketch_two, ranks[1])
    return jnp.einsum("sn,rkn->rks", basis_two, regrouped, precision=HIGHEST)


def dot(a, b, dims):
    return lax.dot_general(
        a, b, (dims, ((), ())), precision=HIGHEST, preferred_element_type=jnp.float32
    )


NN = ((1,), (0,))
NT = ((1,), (1,))
TN = ((0,), (0,))
BLOCK = 8


def inverse_factor(work, linv):
    size = linv.shape[0]
    tile = (BLOCK, size)
    sub = lax.broadcasted_iota(jnp.int32, tile, 0)

    def body(i, carry):
        r0 = pl.multiple_of(i * BLOCK, BLOCK)
        rows_a = work[pl.ds(r0, BLOCK), :size]
        rows_t = work[pl.ds(r0, BLOCK), size:]
        rolled = pltpu.roll(rows_a, lax.rem(size - r0, size), 1)
        d = {}
        for q in range(BLOCK):
            column = jnp.broadcast_to(rolled[:, q : q + 1], tile)
            for p in range(q, BLOCK):
                d[p, q] = jnp.broadcast_to(column[p : p + 1, :], tile)
        done_a, done_t = [], []
        panel_a = jnp.zeros(tile, jnp.float32)
        panel_t = jnp.zeros(tile, jnp.float32)
        for j in range(BLOCK):
            x = d[j, j]
            y = lax.rsqrt(x)
            y = y * (1.5 - 0.5 * ((x * y) * y))
            for p in range(j + 1, BLOCK):
                d[p, j] = d[p, j] * y
            for q in range(j + 1, BLOCK):
                for p in range(q, BLOCK):
                    d[p, q] = d[p, q] - d[p, j] * d[q, j]
            ra = jnp.broadcast_to(rows_a[j : j + 1, :], tile)
            rt = jnp.broadcast_to(rows_t[j : j + 1, :], tile)
            for k in range(j):
                ra = ra - d[j, k] * done_a[k]
                rt = rt - d[j, k] * done_t[k]
            ra = ra * y
            rt = rt * y
            done_a.append(ra)
            done_t.append(rt)
            panel_a = jnp.where(sub == j, ra, panel_a)
            panel_t = jnp.where(sub == j, rt, panel_t)
        linv[pl.ds(r0, BLOCK), :] = panel_t
        both = jnp.concatenate([panel_a, panel_t], axis=1)
        work[...] = work[...] - dot(panel_a, both, TN)
        return carry

    lax.fori_loop(0, size // BLOCK, body, 0)


def fill_work(work, inner, keep_row, size):
    row = lax.broadcasted_iota(jnp.int32, (size, size), 0)
    col = lax.broadcasted_iota(jnp.int32, (size, size), 1)
    eye = (row == col).astype(jnp.float32)
    work[:, :size] = inner + eye * (1.0 - keep_row)
    work[:, size:] = eye


def kernel(
    n, field, sketch_one, sketch_two, ranks, out,
    flat, part_one, pair_one, got_one, full_one, work, linv, core, give, have,
    part_two, pair_two, got_two, full_two, send_sem, recv_sem,
):
    me = lax.axis_index("wide")
    ydev, kdim, n1 = field.shape
    size = sketch_one.shape[1]
    n2 = sketch_two.shape[0]
    stride = flat.shape[0] // ydev
    per = size // n

    barrier = pltpu.get_barrier_semaphore()

    def greet(i, carry):
        peer = lax.rem(me + 1 + i, n)
        pl.semaphore_signal(barrier, inc=1, device_id={"wide": peer}, device_id_type=MESH)
        return carry

    lax.fori_loop(0, n - 1, greet, 0)

    core_id = lax.rem(me, 2)
    chip = me // 2
    chips = n // 2

    def every(i):
        return lax.rem(me + 1 + i, n)

    def alike(i):
        return 2 * lax.rem(chip + 1 + i, chips) + core_id

    def twin(i):
        return chip * 2 + 1 - core_id

    def exchange(phase, count, peer_of, source, target, whole):
        def start(i, carry):
            peer = peer_of(i)
            pltpu.make_async_remote_copy(
                src_ref=source(peer), dst_ref=target(i),
                send_sem=send_sem.at[phase], recv_sem=recv_sem.at[phase],
                device_id={"wide": peer}, device_id_type=MESH,
            ).start()
            return carry

        lax.fori_loop(0, count, start, 0)
        everything = pltpu.make_async_remote_copy(
            src_ref=whole, dst_ref=whole,
            send_sem=send_sem.at[phase], recv_sem=recv_sem.at[phase],
            device_id={"wide": peer_of(0)}, device_id_type=MESH,
        )
        everything.wait_recv()
        everything.wait_send()

    def sum_over_devices(phase, part, pair, got, full):
        rows = part.shape[0]
        half = rows // 2
        chunk = rows // n

        def half_of(device):
            return pl.ds(pl.multiple_of(lax.rem(device, 2) * half, 8), half)

        def chunk_of(device):
            start = lax.rem(device, 2) * half + (device // 2) * chunk
            return pl.ds(pl.multiple_of(start, 8), chunk)

        exchange(phase, 1, twin, lambda p: part.at[half_of(p), :], lambda i: pair, pair)
        mine = half_of(me)
        part[mine, :] = part[mine, :] + pair[...]
        exchange(
            phase + 1, chips - 1, alike,
            lambda p: part.at[chunk_of(p), :], lambda i: got.at[i], got,
        )
        own = chunk_of(me)
        full[own, :] = jnp.sum(got[...], axis=0) + part[own, :]
        exchange(
            phase + 2, chips - 1, alike,
            lambda p: full.at[own, :], lambda i: full.at[own, :],
            full.at[pl.ds(0, half - chunk), :],
        )
        exchange(
            phase + 3, 1, twin,
            lambda p: full.at[mine, :], lambda i: full.at[mine, :],
            full.at[pl.ds(0, half), :],
        )

    lane = lax.broadcasted_iota(jnp.int32, (1, size), 1)
    keep_one = (lane < ranks[0]).astype(jnp.float32)
    keep_two = (lane < ranks[1]).astype(jnp.float32)

    for y in range(ydev):
        flat[y * stride : y * stride + kdim, :] = field[y]
        flat[y * stride + kdim : (y + 1) * stride, :] = jnp.zeros(
            (stride - kdim, n1), jnp.float32
        )
    projected = dot(flat[...], sketch_one[...] * keep_one, NN)
    part_one[...] = dot(projected, flat[...], TN).T
    masked_two = (sketch_two[...] * keep_two).T

    pl.semaphore_wait(barrier, n - 1)

    sum_over_devices(0, part_one, pair_one, got_one, full_one)
    sk = full_one[...]
    fill_work(work, dot(sk, sk, TN), keep_one, size)
    rotated = dot(flat[...], sk, NN)
    inverse_factor(work, linv)
    mixed = dot(linv[...], rotated, NT)
    for t in range(ydev // 2):
        core[t] = mixed[:, 2 * stride * t : 2 * stride * (t + 1)]

    low = lax.broadcasted_iota(jnp.int32, (n, 2 * stride), 1) < stride
    for half in range(per // 2):
        for t in range(ydev // 2):
            first = core[t, pl.ds(2 * half, n, stride=per), :]
            second = core[t, pl.ds(2 * half + 1, n, stride=per), :]
            even = jnp.where(low, first, pltpu.roll(second, stride, 1))
            odd = jnp.where(low, pltpu.roll(first, stride, 1), second)
            give[half, pl.ds(2 * t, n, stride=ydev), :] = even
            give[half, pl.ds(2 * t + 1, n, stride=ydev), :] = odd
    mine_y = pl.ds(pl.multiple_of(me * ydev, ydev), ydev)
    have[:, mine_y, :] = give[:, mine_y, :]
    exchange(
        8, n - 1, every,
        lambda p: give.at[:, pl.ds(pl.multiple_of(p * ydev, ydev), ydev), :],
        lambda i: have.at[:, mine_y, :],
        have.at[:, pl.ds(0, n2 - ydev), :],
    )

    total = jnp.zeros((n2, size), jnp.float32)
    for half in range(per // 2):
        fibers = have[half]
        total = total + dot(fibers, dot(masked_two, fibers, NN), NT)
    part_two[...] = total
    sum_over_devices(4, part_two, pair_two, got_two, full_two)
    sk = full_two[...]
    fill_work(work, dot(sk, sk, TN), keep_two, size)
    spun = [dot(have[half], sk, TN) for half in range(per // 2)]
    inverse_factor(work, linv)
    for half in range(per // 2):
        done = dot(spun[half], linv[...], NT)
        for i in range(2):
            out[2 * half + i] = done[stride * i : stride * i + kdim, :]


def fused(n, field, sketch_one, sketch_two, ranks):
    ydev, kdim, n1 = field.shape
    n2, size = sketch_two.shape
    stride = size // 2
    vmem = pl.BlockSpec(memory_space=pltpu.VMEM)
    f32 = jnp.float32
    return pl.pallas_call(
        functools.partial(kernel, n),
        out_shape=jax.ShapeDtypeStruct((size // n, kdim, size), f32),
        in_specs=[vmem, vmem, vmem, pl.BlockSpec(memory_space=pltpu.SMEM)],
        out_specs=vmem,
        scratch_shapes=[
            pltpu.VMEM((ydev * stride, n1), f32),
            pltpu.VMEM((n1, size), f32),
            pltpu.VMEM((n1 // 2, size), f32),
            pltpu.VMEM((n // 2 - 1, n1 // n, size), f32),
            pltpu.VMEM((n1, size), f32),
            pltpu.VMEM((size, 2 * size), f32),
            pltpu.VMEM((size, size), f32),
            pltpu.VMEM((ydev // 2, size, 2 * stride), f32),
            pltpu.VMEM((size // n // 2, n2, size), f32),
            pltpu.VMEM((size // n // 2, n2, size), f32),
            pltpu.VMEM((n2, size), f32),
            pltpu.VMEM((n2 // 2, size), f32),
            pltpu.VMEM((n // 2 - 1, n2 // n, size), f32),
            pltpu.VMEM((n2, size), f32),
            pltpu.SemaphoreType.DMA((9,)),
            pltpu.SemaphoreType.DMA((9,)),
        ],
        compiler_params=pltpu.CompilerParams(
            collective_id=0, has_side_effects=True, vmem_limit_bytes=32 * 1024 * 1024
        ),
        cost_estimate=pl.CostEstimate(
            flops=600_000_000, bytes_accessed=2_000_000, transcendentals=256
        ),
    )(field, sketch_one, sketch_two, ranks)


def solution(mesh):
    n = mesh.shape["wide"]

    def per_device(field, sketch_one, sketch_two, ranks):
        ydev, kdim, n1 = field.shape
        n2, size = sketch_two.shape
        fits = (
            mesh.shape["narrow"] == 1
            and size == 128
            and n % 2 == 0
            and n >= 4
            and ydev == 8
            and kdim <= size // 2
            and size % (2 * n) == 0
            and n1 % (8 * n) == 0
            and n2 == 8 * n
        )
        if fits:
            return fused(n, field, sketch_one, sketch_two, ranks)
        return general(field, sketch_one, sketch_two, ranks)

    return jax.shard_map(
        per_device,
        mesh=mesh,
        in_specs=(P("wide", "narrow", None), P(), P(), P()),
        out_specs=P("wide", "narrow", None),
        check_vma=False,
    )
```

```python
import functools

import jax
import jax.numpy as jnp
from jax import lax
from jax.experimental import pallas as pl
from jax.experimental.pallas import tpu as pltpu
from jax.sharding import PartitionSpec as P

HIGHEST = lax.Precision.HIGHEST
MESH = pl.DeviceIdType.MESH


def make_basis(local, sketch, rank):
    keep = (jnp.arange(sketch.shape[1]) < rank).astype(jnp.float32)
    masked = sketch * keep
    part = jnp.einsum("akn,ns->aks", local, masked, precision=HIGHEST)
    part = jnp.einsum("akn,aks->ns", local, part, precision=HIGHEST)
    sketched = lax.psum(part, ("wide", "narrow"))
    inner = jnp.dot(sketched.T, sketched, precision=HIGHEST) + jnp.diag(1.0 - keep)
    lower = jnp.linalg.cholesky(inner)
    return jax.scipy.linalg.solve_triangular(lower, sketched.T, lower=True)


def general(field, sketch_one, sketch_two, ranks):
    basis_one = make_basis(field, sketch_one, ranks[0])
    core_one = jnp.einsum("rn,ykn->rky", basis_one, field, precision=HIGHEST)
    regrouped = lax.all_to_all(core_one, "wide", split_axis=0, concat_axis=2, tiled=True)
    basis_two = make_basis(regrouped, sketch_two, ranks[1])
    return jnp.einsum("sn,rkn->rks", basis_two, regrouped, precision=HIGHEST)


def dot(a, b, dims):
    return lax.dot_general(
        a, b, (dims, ((), ())), precision=HIGHEST, preferred_element_type=jnp.float32
    )


NN = ((1,), (0,))
NT = ((1,), (1,))
TN = ((0,), (0,))
BLOCK = 8
TILES = 4


def inverse_factor(work, linv):
    size = linv.shape[0]
    tile = (BLOCK, size)
    group = TILES * BLOCK
    sub = lax.broadcasted_iota(jnp.int32, tile, 0)

    def body(i, carry):
        r0 = pl.multiple_of(i * group, group)
        rolled = pltpu.roll(
            work[pl.ds(r0, group), :size], lax.rem(size - r0, size), 1
        )
        rest = work[pl.ds(r0, group), size:]
        rows_a = [rolled[u * BLOCK : (u + 1) * BLOCK, :] for u in range(TILES)]
        rows_t = [rest[u * BLOCK : (u + 1) * BLOCK, :] for u in range(TILES)]
        panels_a, panels_t = [], []
        for u in range(TILES):
            d, below = {}, {}
            for q in range(BLOCK):
                lane = u * BLOCK + q
                column = jnp.broadcast_to(rows_a[u][:, lane : lane + 1], tile)
                for p in range(q, BLOCK):
                    d[p, q] = jnp.broadcast_to(column[p : p + 1, :], tile)
                for v in range(u + 1, TILES):
                    below[v, q] = jnp.broadcast_to(rows_a[v][:, lane : lane + 1], tile)
            done_a, done_t = [], []
            panel_a = jnp.zeros(tile, jnp.float32)
            panel_t = jnp.zeros(tile, jnp.float32)
            for j in range(BLOCK):
                x = d[j, j]
                y = lax.rsqrt(x)
                y = y * (1.5 - 0.5 * ((x * y) * y))
                for p in range(j + 1, BLOCK):
                    d[p, j] = d[p, j] * y
                for v in range(u + 1, TILES):
                    below[v, j] = below[v, j] * y
                for q in range(j + 1, BLOCK):
                    for p in range(q, BLOCK):
                        d[p, q] = d[p, q] - d[p, j] * d[q, j]
                    for v in range(u + 1, TILES):
                        below[v, q] = below[v, q] - below[v, j] * d[q, j]
                ra = jnp.broadcast_to(rows_a[u][j : j + 1, :], tile)
                rt = jnp.broadcast_to(rows_t[u][j : j + 1, :], tile)
                for k in range(j):
                    ra = ra - d[j, k] * done_a[k]
                    rt = rt - d[j, k] * done_t[k]
                ra = ra * y
                rt = rt * y
                done_a.append(ra)
                done_t.append(rt)
                panel_a = jnp.where(sub == j, ra, panel_a)
                panel_t = jnp.where(sub == j, rt, panel_t)
                for v in range(u + 1, TILES):
                    rows_a[v] = rows_a[v] - below[v, j] * ra
                    rows_t[v] = rows_t[v] - below[v, j] * rt
            panels_a.append(panel_a)
            panels_t.append(panel_t)
        panel_t = jnp.concatenate(panels_t, axis=0)
        panel_a = pltpu.roll(jnp.concatenate(panels_a, axis=0), r0, 1)
        linv[pl.ds(r0, group), :] = panel_t
        both = jnp.concatenate([panel_a, panel_t], axis=1)
        work[...] = work[...] - dot(panel_a, both, TN)
        return carry

    lax.fori_loop(0, size // group, body, 0)


def fill_work(work, inner, keep_row, size):
    row = lax.broadcasted_iota(jnp.int32, (size, size), 0)
    col = lax.broadcasted_iota(jnp.int32, (size, size), 1)
    eye = (row == col).astype(jnp.float32)
    work[:, :size] = inner + eye * (1.0 - keep_row)
    work[:, size:] = eye


def kernel(
    n, field, sketch_one, sketch_two, ranks, out,
    flat, part_one, pair_one, got_one, full_one, work, linv, core, give, have,
    part_two, pair_two, got_two, full_two, send_sem, recv_sem,
):
    me = lax.axis_index("wide")
    ydev, kdim, n1 = field.shape
    size = sketch_one.shape[1]
    n2 = sketch_two.shape[0]
    stride = flat.shape[0] // ydev
    per = size // n

    barrier = pltpu.get_barrier_semaphore()

    def greet(i, carry):
        peer = lax.rem(me + 1 + i, n)
        pl.semaphore_signal(barrier, inc=1, device_id={"wide": peer}, device_id_type=MESH)
        return carry

    lax.fori_loop(0, n - 1, greet, 0)

    core_id = lax.rem(me, 2)
    chip = me // 2
    chips = n // 2

    def every(i):
        return lax.rem(me + 1 + i, n)

    def alike(i):
        return 2 * lax.rem(chip + 1 + i, chips) + core_id

    def twin(i):
        return chip * 2 + 1 - core_id

    def exchange(phase, count, peer_of, source, target, whole):
        def start(i, carry):
            peer = peer_of(i)
            pltpu.make_async_remote_copy(
                src_ref=source(peer), dst_ref=target(i),
                send_sem=send_sem.at[phase], recv_sem=recv_sem.at[phase],
                device_id={"wide": peer}, device_id_type=MESH,
            ).start()
            return carry

        lax.fori_loop(0, count, start, 0)
        everything = pltpu.make_async_remote_copy(
            src_ref=whole, dst_ref=whole,
            send_sem=send_sem.at[phase], recv_sem=recv_sem.at[phase],
            device_id={"wide": peer_of(0)}, device_id_type=MESH,
        )
        everything.wait_recv()
        everything.wait_send()

    def sum_over_devices(phase, part, pair, got, full):
        rows = part.shape[0]
        half = rows // 2
        chunk = rows // n

        def half_of(device):
            return pl.ds(pl.multiple_of(lax.rem(device, 2) * half, 8), half)

        def chunk_of(device):
            start = lax.rem(device, 2) * half + (device // 2) * chunk
            return pl.ds(pl.multiple_of(start, 8), chunk)

        exchange(phase, 1, twin, lambda p: part.at[half_of(p), :], lambda i: pair, pair)
        mine = half_of(me)
        part[mine, :] = part[mine, :] + pair[...]
        exchange(
            phase + 1, chips - 1, alike,
            lambda p: part.at[chunk_of(p), :], lambda i: got.at[i], got,
        )
        own = chunk_of(me)
        full[own, :] = jnp.sum(got[...], axis=0) + part[own, :]
        exchange(
            phase + 2, chips - 1, alike,
            lambda p: full.at[own, :], lambda i: full.at[own, :],
            full.at[pl.ds(0, half - chunk), :],
        )
        exchange(
            phase + 3, 1, twin,
            lambda p: full.at[mine, :], lambda i: full.at[mine, :],
            full.at[pl.ds(0, half), :],
        )

    lane = lax.broadcasted_iota(jnp.int32, (1, size), 1)
    keep_one = (lane < ranks[0]).astype(jnp.float32)
    keep_two = (lane < ranks[1]).astype(jnp.float32)

    for y in range(ydev):
        flat[y * stride : y * stride + kdim, :] = field[y]
        flat[y * stride + kdim : (y + 1) * stride, :] = jnp.zeros(
            (stride - kdim, n1), jnp.float32
        )
    projected = dot(flat[...], sketch_one[...] * keep_one, NN)
    part_one[...] = dot(projected, flat[...], TN).T
    masked_two = (sketch_two[...] * keep_two).T

    pl.semaphore_wait(barrier, n - 1)

    sum_over_devices(0, part_one, pair_one, got_one, full_one)
    sk = full_one[...]
    fill_work(work, dot(sk, sk, TN), keep_one, size)
    rotated = dot(flat[...], sk, NN)
    inverse_factor(work, linv)
    mixed = dot(linv[...], rotated, NT)
    for t in range(ydev // 2):
        core[t] = mixed[:, 2 * stride * t : 2 * stride * (t + 1)]

    low = lax.broadcasted_iota(jnp.int32, (n, 2 * stride), 1) < stride
    for half in range(per // 2):
        for t in range(ydev // 2):
            first = core[t, pl.ds(2 * half, n, stride=per), :]
            second = core[t, pl.ds(2 * half + 1, n, stride=per), :]
            even = jnp.where(low, first, pltpu.roll(second, stride, 1))
            odd = jnp.where(low, pltpu.roll(first, stride, 1), second)
            give[half, pl.ds(2 * t, n, stride=ydev), :] = even
            give[half, pl.ds(2 * t + 1, n, stride=ydev), :] = odd
    mine_y = pl.ds(pl.multiple_of(me * ydev, ydev), ydev)
    have[:, mine_y, :] = give[:, mine_y, :]
    exchange(
        8, n - 1, every,
        lambda p: give.at[:, pl.ds(pl.multiple_of(p * ydev, ydev), ydev), :],
        lambda i: have.at[:, mine_y, :],
        have.at[:, pl.ds(0, n2 - ydev), :],
    )

    total = jnp.zeros((n2, size), jnp.float32)
    for half in range(per // 2):
        fibers = have[half]
        total = total + dot(fibers, dot(masked_two, fibers, NN), NT)
    part_two[...] = total
    sum_over_devices(4, part_two, pair_two, got_two, full_two)
    sk = full_two[...]
    fill_work(work, dot(sk, sk, TN), keep_two, size)
    spun = [dot(have[half], sk, TN) for half in range(per // 2)]
    inverse_factor(work, linv)
    for half in range(per // 2):
        done = dot(spun[half], linv[...], NT)
        for i in range(2):
            out[2 * half + i] = done[stride * i : stride * i + kdim, :]


def fused(n, field, sketch_one, sketch_two, ranks):
    ydev, kdim, n1 = field.shape
    n2, size = sketch_two.shape
    stride = size // 2
    vmem = pl.BlockSpec(memory_space=pltpu.VMEM)
    f32 = jnp.float32
    return pl.pallas_call(
        functools.partial(kernel, n),
        out_shape=jax.ShapeDtypeStruct((size // n, kdim, size), f32),
        in_specs=[vmem, vmem, vmem, pl.BlockSpec(memory_space=pltpu.SMEM)],
        out_specs=vmem,
        scratch_shapes=[
            pltpu.VMEM((ydev * stride, n1), f32),
            pltpu.VMEM((n1, size), f32),
            pltpu.VMEM((n1 // 2, size), f32),
            pltpu.VMEM((n // 2 - 1, n1 // n, size), f32),
            pltpu.VMEM((n1, size), f32),
            pltpu.VMEM((size, 2 * size), f32),
            pltpu.VMEM((size, size), f32),
            pltpu.VMEM((ydev // 2, size, 2 * stride), f32),
            pltpu.VMEM((size // n // 2, n2, size), f32),
            pltpu.VMEM((size // n // 2, n2, size), f32),
            pltpu.VMEM((n2, size), f32),
            pltpu.VMEM((n2 // 2, size), f32),
            pltpu.VMEM((n // 2 - 1, n2 // n, size), f32),
            pltpu.VMEM((n2, size), f32),
            pltpu.SemaphoreType.DMA((9,)),
            pltpu.SemaphoreType.DMA((9,)),
        ],
        compiler_params=pltpu.CompilerParams(
            collective_id=0, has_side_effects=True, vmem_limit_bytes=32 * 1024 * 1024
        ),
        cost_estimate=pl.CostEstimate(
            flops=600_000_000, bytes_accessed=2_000_000, transcendentals=256
        ),
    )(field, sketch_one, sketch_two, ranks)


def solution(mesh):
    n = mesh.shape["wide"]

    def per_device(field, sketch_one, sketch_two, ranks):
        ydev, kdim, n1 = field.shape
        n2, size = sketch_two.shape
        fits = (
            mesh.shape["narrow"] == 1
            and size == 128
            and n % 2 == 0
            and n >= 4
            and ydev == 8
            and kdim <= size // 2
            and size % (2 * n) == 0
            and n1 % (8 * n) == 0
            and n2 == 8 * n
        )
        if fits:
            return fused(n, field, sketch_one, sketch_two, ranks)
        return general(field, sketch_one, sketch_two, ranks)

    return jax.shard_map(
        per_device,
        mesh=mesh,
        in_specs=(P("wide", "narrow", None), P(), P(), P()),
        out_specs=P("wide", "narrow", None),
        check_vma=False,
    )
```

```python
import functools

import jax
import jax.numpy as jnp
from jax import lax
from jax.experimental import pallas as pl
from jax.experimental.pallas import tpu as pltpu
from jax.sharding import PartitionSpec as P

HIGHEST = lax.Precision.HIGHEST
MESH = pl.DeviceIdType.MESH


def make_basis(local, sketch, rank):
    keep = (jnp.arange(sketch.shape[1]) < rank).astype(jnp.float32)
    masked = sketch * keep
    part = jnp.einsum("akn,ns->aks", local, masked, precision=HIGHEST)
    part = jnp.einsum("akn,aks->ns", local, part, precision=HIGHEST)
    sketched = lax.psum(part, ("wide", "narrow"))
    inner = jnp.dot(sketched.T, sketched, precision=HIGHEST) + jnp.diag(1.0 - keep)
    lower = jnp.linalg.cholesky(inner)
    return jax.scipy.linalg.solve_triangular(lower, sketched.T, lower=True)


def general(field, sketch_one, sketch_two, ranks):
    basis_one = make_basis(field, sketch_one, ranks[0])
    core_one = jnp.einsum("rn,ykn->rky", basis_one, field, precision=HIGHEST)
    regrouped = lax.all_to_all(core_one, "wide", split_axis=0, concat_axis=2, tiled=True)
    basis_two = make_basis(regrouped, sketch_two, ranks[1])
    return jnp.einsum("sn,rkn->rks", basis_two, regrouped, precision=HIGHEST)


def dot(a, b, dims):
    return lax.dot_general(
        a, b, (dims, ((), ())), precision=HIGHEST, preferred_element_type=jnp.float32
    )


NN = ((1,), (0,))
NT = ((1,), (1,))
TN = ((0,), (0,))
BLOCK = 8
TILES = 4


def inverse_factor(work, linv):
    size = linv.shape[0]
    tile = (BLOCK, size)
    group = TILES * BLOCK
    sub = lax.broadcasted_iota(jnp.int32, tile, 0)

    for r0 in range(0, size, group):
        own = work[r0 : r0 + group, :size]
        rest = work[r0 : r0 + group, size:]
        rows_a = [own[u * BLOCK : (u + 1) * BLOCK, :] for u in range(TILES)]
        rows_t = [rest[u * BLOCK : (u + 1) * BLOCK, :] for u in range(TILES)]
        panels_a, panels_t = [], []
        for u in range(TILES):
            d, below = {}, {}
            for q in range(BLOCK):
                lane = r0 + u * BLOCK + q
                column = jnp.broadcast_to(rows_a[u][:, lane : lane + 1], tile)
                for p in range(q, BLOCK):
                    d[p, q] = jnp.broadcast_to(column[p : p + 1, :], tile)
                for v in range(u + 1, TILES):
                    below[v, q] = jnp.broadcast_to(rows_a[v][:, lane : lane + 1], tile)
            done_a, done_t = [], []
            panel_a = jnp.zeros(tile, jnp.float32)
            panel_t = jnp.zeros(tile, jnp.float32)
            for j in range(BLOCK):
                x = d[j, j]
                y = lax.rsqrt(x)
                y = y * (1.5 - 0.5 * ((x * y) * y))
                for p in range(j + 1, BLOCK):
                    d[p, j] = d[p, j] * y
                for v in range(u + 1, TILES):
                    below[v, j] = below[v, j] * y
                for q in range(j + 1, BLOCK):
                    for p in range(q, BLOCK):
                        d[p, q] = d[p, q] - d[p, j] * d[q, j]
                    for v in range(u + 1, TILES):
                        below[v, q] = below[v, q] - below[v, j] * d[q, j]
                ra = jnp.broadcast_to(rows_a[u][j : j + 1, :], tile)
                rt = jnp.broadcast_to(rows_t[u][j : j + 1, :], tile)
                for k in range(j):
                    ra = ra - d[j, k] * done_a[k]
                    rt = rt - d[j, k] * done_t[k]
                ra = ra * y
                rt = rt * y
                done_a.append(ra)
                done_t.append(rt)
                panel_a = jnp.where(sub == j, ra, panel_a)
                panel_t = jnp.where(sub == j, rt, panel_t)
                for v in range(u + 1, TILES):
                    rows_a[v] = rows_a[v] - below[v, j] * ra
                    rows_t[v] = rows_t[v] - below[v, j] * rt
            panels_a.append(panel_a)
            panels_t.append(panel_t)
        panel_t = jnp.concatenate(panels_t, axis=0)
        panel_a = jnp.concatenate(panels_a, axis=0)
        linv[r0 : r0 + group, :] = panel_t
        end = r0 + group
        if end < size:
            both = jnp.concatenate([panel_a, panel_t], axis=1)
            work[end:, :] = work[end:, :] - dot(panel_a.T[end:, :], both, NN)


def fill_work(work, inner, keep_row, size):
    row = lax.broadcasted_iota(jnp.int32, (size, size), 0)
    col = lax.broadcasted_iota(jnp.int32, (size, size), 1)
    eye = (row == col).astype(jnp.float32)
    work[:, :size] = inner + eye * (1.0 - keep_row)
    work[:, size:] = eye


def kernel(
    n, field, sketch_one, sketch_two, ranks, out,
    flat, part_one, pair_one, got_one, full_one, work, linv, core, give, have,
    part_two, pair_two, got_two, full_two, send_sem, recv_sem,
):
    me = lax.axis_index("wide")
    ydev, kdim, n1 = field.shape
    size = sketch_one.shape[1]
    n2 = sketch_two.shape[0]
    stride = flat.shape[0] // ydev
    per = size // n

    barrier = pltpu.get_barrier_semaphore()

    def greet(i, carry):
        peer = lax.rem(me + 1 + i, n)
        pl.semaphore_signal(barrier, inc=1, device_id={"wide": peer}, device_id_type=MESH)
        return carry

    lax.fori_loop(0, n - 1, greet, 0)

    core_id = lax.rem(me, 2)
    chip = me // 2
    chips = n // 2

    def every(i):
        return lax.rem(me + 1 + i, n)

    def alike(i):
        return 2 * lax.rem(chip + 1 + i, chips) + core_id

    def twin(i):
        return chip * 2 + 1 - core_id

    def exchange(phase, count, peer_of, source, target, whole):
        def start(i, carry):
            peer = peer_of(i)
            pltpu.make_async_remote_copy(
                src_ref=source(peer), dst_ref=target(i),
                send_sem=send_sem.at[phase], recv_sem=recv_sem.at[phase],
                device_id={"wide": peer}, device_id_type=MESH,
            ).start()
            return carry

        lax.fori_loop(0, count, start, 0)
        everything = pltpu.make_async_remote_copy(
            src_ref=whole, dst_ref=whole,
            send_sem=send_sem.at[phase], recv_sem=recv_sem.at[phase],
            device_id={"wide": peer_of(0)}, device_id_type=MESH,
        )
        everything.wait_recv()
        everything.wait_send()

    def sum_over_devices(phase, part, pair, got, full, direct):
        rows = part.shape[0]
        half = rows // 2
        chunk = rows // n

        def half_of(device):
            return pl.ds(pl.multiple_of(lax.rem(device, 2) * half, 8), half)

        def chunk_of(device):
            start = lax.rem(device, 2) * half + (device // 2) * chunk
            return pl.ds(pl.multiple_of(start, 8), chunk)

        exchange(phase, 1, twin, lambda p: part.at[half_of(p), :], lambda i: pair, pair)
        mine = half_of(me)
        part[mine, :] = part[mine, :] + pair[...]
        exchange(
            phase + 1, chips - 1, alike,
            lambda p: part.at[chunk_of(p), :], lambda i: got.at[i], got,
        )
        own = chunk_of(me)
        full[own, :] = jnp.sum(got[...], axis=0) + part[own, :]
        if direct:
            exchange(
                phase + 2, n - 1, every,
                lambda p: full.at[own, :], lambda i: full.at[own, :],
                full.at[pl.ds(0, rows - chunk), :],
            )
            return
        exchange(
            phase + 2, chips - 1, alike,
            lambda p: full.at[own, :], lambda i: full.at[own, :],
            full.at[pl.ds(0, half - chunk), :],
        )
        exchange(
            phase + 3, 1, twin,
            lambda p: full.at[mine, :], lambda i: full.at[mine, :],
            full.at[pl.ds(0, half), :],
        )

    lane = lax.broadcasted_iota(jnp.int32, (1, size), 1)
    keep_one = (lane < ranks[0]).astype(jnp.float32)
    keep_two = (lane < ranks[1]).astype(jnp.float32)

    for y in range(ydev):
        flat[y * stride : y * stride + kdim, :] = field[y]
        flat[y * stride + kdim : (y + 1) * stride, :] = jnp.zeros(
            (stride - kdim, n1), jnp.float32
        )
    projected = dot(flat[...], sketch_one[...] * keep_one, NN)
    part_one[...] = dot(projected, flat[...], TN).T
    masked_two = (sketch_two[...] * keep_two).T

    pl.semaphore_wait(barrier, n - 1)

    sum_over_devices(0, part_one, pair_one, got_one, full_one, False)
    sk = full_one[...]
    fill_work(work, dot(sk, sk, TN), keep_one, size)
    rotated = dot(flat[...], sk, NN)
    inverse_factor(work, linv)
    mixed = dot(linv[...], rotated, NT)
    for t in range(ydev // 2):
        core[t] = mixed[:, 2 * stride * t : 2 * stride * (t + 1)]

    low = lax.broadcasted_iota(jnp.int32, (n, 2 * stride), 1) < stride
    for half in range(per // 2):
        for t in range(ydev // 2):
            first = core[t, pl.ds(2 * half, n, stride=per), :]
            second = core[t, pl.ds(2 * half + 1, n, stride=per), :]
            even = jnp.where(low, first, pltpu.roll(second, stride, 1))
            odd = jnp.where(low, pltpu.roll(first, stride, 1), second)
            give[half, pl.ds(2 * t, n, stride=ydev), :] = even
            give[half, pl.ds(2 * t + 1, n, stride=ydev), :] = odd
    mine_y = pl.ds(pl.multiple_of(me * ydev, ydev), ydev)
    have[:, mine_y, :] = give[:, mine_y, :]
    exchange(
        8, n - 1, every,
        lambda p: give.at[:, pl.ds(pl.multiple_of(p * ydev, ydev), ydev), :],
        lambda i: have.at[:, mine_y, :],
        have.at[:, pl.ds(0, n2 - ydev), :],
    )

    total = jnp.zeros((n2, size), jnp.float32)
    for half in range(per // 2):
        fibers = have[half]
        total = total + dot(fibers, dot(masked_two, fibers, NN), NT)
    part_two[...] = total
    sum_over_devices(4, part_two, pair_two, got_two, full_two, True)
    sk = full_two[...]
    fill_work(work, dot(sk, sk, TN), keep_two, size)
    spun = [dot(have[half], sk, TN) for half in range(per // 2)]
    inverse_factor(work, linv)
    for half in range(per // 2):
        done = dot(spun[half], linv[...], NT)
        for i in range(2):
            out[2 * half + i] = done[stride * i : stride * i + kdim, :]


def fused(n, field, sketch_one, sketch_two, ranks):
    ydev, kdim, n1 = field.shape
    n2, size = sketch_two.shape
    stride = size // 2
    vmem = pl.BlockSpec(memory_space=pltpu.VMEM)
    f32 = jnp.float32
    return pl.pallas_call(
        functools.partial(kernel, n),
        out_shape=jax.ShapeDtypeStruct((size // n, kdim, size), f32),
        in_specs=[vmem, vmem, vmem, pl.BlockSpec(memory_space=pltpu.SMEM)],
        out_specs=vmem,
        scratch_shapes=[
            pltpu.VMEM((ydev * stride, n1), f32),
            pltpu.VMEM((n1, size), f32),
            pltpu.VMEM((n1 // 2, size), f32),
            pltpu.VMEM((n // 2 - 1, n1 // n, size), f32),
            pltpu.VMEM((n1, size), f32),
            pltpu.VMEM((size, 2 * size), f32),
            pltpu.VMEM((size, size), f32),
            pltpu.VMEM((ydev // 2, size, 2 * stride), f32),
            pltpu.VMEM((size // n // 2, n2, size), f32),
            pltpu.VMEM((size // n // 2, n2, size), f32),
            pltpu.VMEM((n2, size), f32),
            pltpu.VMEM((n2 // 2, size), f32),
            pltpu.VMEM((n // 2 - 1, n2 // n, size), f32),
            pltpu.VMEM((n2, size), f32),
            pltpu.SemaphoreType.DMA((9,)),
            pltpu.SemaphoreType.DMA((9,)),
        ],
        compiler_params=pltpu.CompilerParams(
            collective_id=0, has_side_effects=True, vmem_limit_bytes=32 * 1024 * 1024
        ),
        cost_estimate=pl.CostEstimate(
            flops=600_000_000, bytes_accessed=2_000_000, transcendentals=256
        ),
    )(field, sketch_one, sketch_two, ranks)


def solution(mesh):
    n = mesh.shape["wide"]

    def per_device(field, sketch_one, sketch_two, ranks):
        ydev, kdim, n1 = field.shape
        n2, size = sketch_two.shape
        fits = (
            mesh.shape["narrow"] == 1
            and size == 128
            and n % 2 == 0
            and n >= 4
            and ydev == 8
            and kdim <= size // 2
            and size % (2 * n) == 0
            and n1 % (8 * n) == 0
            and n2 == 8 * n
        )
        if fits:
            return fused(n, field, sketch_one, sketch_two, ranks)
        return general(field, sketch_one, sketch_two, ranks)

    return jax.shard_map(
        per_device,
        mesh=mesh,
        in_specs=(P("wide", "narrow", None), P(), P(), P()),
        out_specs=P("wide", "narrow", None),
        check_vma=False,
    )
```

```python
import functools

import jax
import jax.numpy as jnp
from jax import lax
from jax.experimental import pallas as pl
from jax.experimental.pallas import tpu as pltpu
from jax.sharding import PartitionSpec as P

HIGHEST = lax.Precision.HIGHEST
MESH = pl.DeviceIdType.MESH


def make_basis(local, sketch, rank):
    keep = (jnp.arange(sketch.shape[1]) < rank).astype(jnp.float32)
    masked = sketch * keep
    part = jnp.einsum("akn,ns->aks", local, masked, precision=HIGHEST)
    part = jnp.einsum("akn,aks->ns", local, part, precision=HIGHEST)
    sketched = lax.psum(part, ("wide", "narrow"))
    inner = jnp.dot(sketched.T, sketched, precision=HIGHEST) + jnp.diag(1.0 - keep)
    lower = jnp.linalg.cholesky(inner)
    return jax.scipy.linalg.solve_triangular(lower, sketched.T, lower=True)


def general(field, sketch_one, sketch_two, ranks):
    basis_one = make_basis(field, sketch_one, ranks[0])
    core_one = jnp.einsum("rn,ykn->rky", basis_one, field, precision=HIGHEST)
    regrouped = lax.all_to_all(core_one, "wide", split_axis=0, concat_axis=2, tiled=True)
    basis_two = make_basis(regrouped, sketch_two, ranks[1])
    return jnp.einsum("sn,rkn->rks", basis_two, regrouped, precision=HIGHEST)


def dot(a, b, dims):
    return lax.dot_general(
        a, b, (dims, ((), ())), precision=HIGHEST, preferred_element_type=jnp.float32
    )


NN = ((1,), (0,))
NT = ((1,), (1,))
TN = ((0,), (0,))
BLOCK = 8
TILES = 8


def inverse_factor(work, linv):
    size = linv.shape[0]
    tile = (BLOCK, size)
    group = TILES * BLOCK
    sub = lax.broadcasted_iota(jnp.int32, tile, 0)

    for r0 in range(0, size, group):
        own = work[r0 : r0 + group, :size]
        rest = work[r0 : r0 + group, size:]
        rows_a = [own[u * BLOCK : (u + 1) * BLOCK, :] for u in range(TILES)]
        rows_t = [rest[u * BLOCK : (u + 1) * BLOCK, :] for u in range(TILES)]
        panels_a, panels_t = [], []
        for u in range(TILES):
            d, below = {}, {}
            for q in range(BLOCK):
                lane = r0 + u * BLOCK + q
                column = jnp.broadcast_to(rows_a[u][:, lane : lane + 1], tile)
                for p in range(q, BLOCK):
                    d[p, q] = jnp.broadcast_to(column[p : p + 1, :], tile)
                for v in range(u + 1, TILES):
                    below[v, q] = jnp.broadcast_to(rows_a[v][:, lane : lane + 1], tile)
            done_a, done_t = [], []
            panel_a = jnp.zeros(tile, jnp.float32)
            panel_t = jnp.zeros(tile, jnp.float32)
            for j in range(BLOCK):
                x = d[j, j]
                y = lax.rsqrt(x)
                y = y * (1.5 - 0.5 * ((x * y) * y))
                for p in range(j + 1, BLOCK):
                    d[p, j] = d[p, j] * y
                for v in range(u + 1, TILES):
                    below[v, j] = below[v, j] * y
                for q in range(j + 1, BLOCK):
                    for p in range(q, BLOCK):
                        d[p, q] = d[p, q] - d[p, j] * d[q, j]
                    for v in range(u + 1, TILES):
                        below[v, q] = below[v, q] - below[v, j] * d[q, j]
                ra = jnp.broadcast_to(rows_a[u][j : j + 1, :], tile)
                rt = jnp.broadcast_to(rows_t[u][j : j + 1, :], tile)
                for k in range(j):
                    ra = ra - d[j, k] * done_a[k]
                    rt = rt - d[j, k] * done_t[k]
                ra = ra * y
                rt = rt * y
                done_a.append(ra)
                done_t.append(rt)
                panel_a = jnp.where(sub == j, ra, panel_a)
                panel_t = jnp.where(sub == j, rt, panel_t)
                for v in range(u + 1, TILES):
                    rows_a[v] = rows_a[v] - below[v, j] * ra
                    rows_t[v] = rows_t[v] - below[v, j] * rt
            panels_a.append(panel_a)
            panels_t.append(panel_t)
        panel_t = jnp.concatenate(panels_t, axis=0)
        panel_a = jnp.concatenate(panels_a, axis=0)
        linv[r0 : r0 + group, :] = panel_t
        end = r0 + group
        if end < size:
            both = jnp.concatenate([panel_a, panel_t], axis=1)
            work[end:, :] = work[end:, :] - dot(panel_a.T[end:, :], both, NN)


def fill_work(work, inner, keep_row, size):
    row = lax.broadcasted_iota(jnp.int32, (size, size), 0)
    col = lax.broadcasted_iota(jnp.int32, (size, size), 1)
    eye = (row == col).astype(jnp.float32)
    work[:, :size] = inner + eye * (1.0 - keep_row)
    work[:, size:] = eye


def kernel(
    n, field, sketch_one, sketch_two, ranks, out,
    flat, part_one, pair_one, got_one, full_one, work, linv, core, give, have,
    part_two, pair_two, got_two, full_two, send_sem, recv_sem,
):
    me = lax.axis_index("wide")
    ydev, kdim, n1 = field.shape
    size = sketch_one.shape[1]
    n2 = sketch_two.shape[0]
    stride = flat.shape[0] // ydev
    per = size // n

    barrier = pltpu.get_barrier_semaphore()

    def greet(i, carry):
        peer = lax.rem(me + 1 + i, n)
        pl.semaphore_signal(barrier, inc=1, device_id={"wide": peer}, device_id_type=MESH)
        return carry

    lax.fori_loop(0, n - 1, greet, 0)

    core_id = lax.rem(me, 2)
    chip = me // 2
    chips = n // 2

    def every(i):
        return lax.rem(me + 1 + i, n)

    def alike(i):
        return 2 * lax.rem(chip + 1 + i, chips) + core_id

    def twin(i):
        return chip * 2 + 1 - core_id

    def exchange(phase, count, peer_of, source, target, whole):
        def start(i, carry):
            peer = peer_of(i)
            pltpu.make_async_remote_copy(
                src_ref=source(peer), dst_ref=target(i),
                send_sem=send_sem.at[phase], recv_sem=recv_sem.at[phase],
                device_id={"wide": peer}, device_id_type=MESH,
            ).start()
            return carry

        lax.fori_loop(0, count, start, 0)
        everything = pltpu.make_async_remote_copy(
            src_ref=whole, dst_ref=whole,
            send_sem=send_sem.at[phase], recv_sem=recv_sem.at[phase],
            device_id={"wide": peer_of(0)}, device_id_type=MESH,
        )
        everything.wait_recv()
        everything.wait_send()

    def sum_over_devices(phase, part, pair, got, full, direct):
        rows = part.shape[0]
        half = rows // 2
        chunk = rows // n

        def half_of(device):
            return pl.ds(pl.multiple_of(lax.rem(device, 2) * half, 8), half)

        def chunk_of(device):
            start = lax.rem(device, 2) * half + (device // 2) * chunk
            return pl.ds(pl.multiple_of(start, 8), chunk)

        exchange(phase, 1, twin, lambda p: part.at[half_of(p), :], lambda i: pair, pair)
        mine = half_of(me)
        part[mine, :] = part[mine, :] + pair[...]
        exchange(
            phase + 1, chips - 1, alike,
            lambda p: part.at[chunk_of(p), :], lambda i: got.at[i], got,
        )
        own = chunk_of(me)
        full[own, :] = jnp.sum(got[...], axis=0) + part[own, :]
        if direct:
            exchange(
                phase + 2, n - 1, every,
                lambda p: full.at[own, :], lambda i: full.at[own, :],
                full.at[pl.ds(0, rows - chunk), :],
            )
            return
        exchange(
            phase + 2, chips - 1, alike,
            lambda p: full.at[own, :], lambda i: full.at[own, :],
            full.at[pl.ds(0, half - chunk), :],
        )
        exchange(
            phase + 3, 1, twin,
            lambda p: full.at[mine, :], lambda i: full.at[mine, :],
            full.at[pl.ds(0, half), :],
        )

    lane = lax.broadcasted_iota(jnp.int32, (1, size), 1)
    keep_one = (lane < ranks[0]).astype(jnp.float32)
    keep_two = (lane < ranks[1]).astype(jnp.float32)

    for y in range(ydev):
        flat[y * stride : y * stride + kdim, :] = field[y]
        flat[y * stride + kdim : (y + 1) * stride, :] = jnp.zeros(
            (stride - kdim, n1), jnp.float32
        )
    projected = dot(flat[...], sketch_one[...] * keep_one, NN)
    part_one[...] = dot(projected, flat[...], TN).T
    masked_two = (sketch_two[...] * keep_two).T

    pl.semaphore_wait(barrier, n - 1)

    sum_over_devices(0, part_one, pair_one, got_one, full_one, False)
    sk = full_one[...]
    fill_work(work, dot(sk, sk, TN), keep_one, size)
    rotated = dot(flat[...], sk, NN)
    inverse_factor(work, linv)
    mixed = dot(linv[...], rotated, NT)
    for t in range(ydev // 2):
        core[t] = mixed[:, 2 * stride * t : 2 * stride * (t + 1)]

    low = lax.broadcasted_iota(jnp.int32, (n, 2 * stride), 1) < stride
    for half in range(per // 2):
        for t in range(ydev // 2):
            first = core[t, pl.ds(2 * half, n, stride=per), :]
            second = core[t, pl.ds(2 * half + 1, n, stride=per), :]
            even = jnp.where(low, first, pltpu.roll(second, stride, 1))
            odd = jnp.where(low, pltpu.roll(first, stride, 1), second)
            give[half, pl.ds(2 * t, n, stride=ydev), :] = even
            give[half, pl.ds(2 * t + 1, n, stride=ydev), :] = odd
    mine_y = pl.ds(pl.multiple_of(me * ydev, ydev), ydev)
    have[:, mine_y, :] = give[:, mine_y, :]
    exchange(
        8, n - 1, every,
        lambda p: give.at[:, pl.ds(pl.multiple_of(p * ydev, ydev), ydev), :],
        lambda i: have.at[:, mine_y, :],
        have.at[:, pl.ds(0, n2 - ydev), :],
    )

    total = jnp.zeros((n2, size), jnp.float32)
    for half in range(per // 2):
        fibers = have[half]
        total = total + dot(fibers, dot(masked_two, fibers, NN), NT)
    part_two[...] = total
    sum_over_devices(4, part_two, pair_two, got_two, full_two, True)
    sk = full_two[...]
    fill_work(work, dot(sk, sk, TN), keep_two, size)
    spun = [dot(have[half], sk, TN) for half in range(per // 2)]
    inverse_factor(work, linv)
    for half in range(per // 2):
        done = dot(spun[half], linv[...], NT)
        for i in range(2):
            out[2 * half + i] = done[stride * i : stride * i + kdim, :]


def fused(n, field, sketch_one, sketch_two, ranks):
    ydev, kdim, n1 = field.shape
    n2, size = sketch_two.shape
    stride = size // 2
    vmem = pl.BlockSpec(memory_space=pltpu.VMEM)
    f32 = jnp.float32
    return pl.pallas_call(
        functools.partial(kernel, n),
        out_shape=jax.ShapeDtypeStruct((size // n, kdim, size), f32),
        in_specs=[vmem, vmem, vmem, pl.BlockSpec(memory_space=pltpu.SMEM)],
        out_specs=vmem,
        scratch_shapes=[
            pltpu.VMEM((ydev * stride, n1), f32),
            pltpu.VMEM((n1, size), f32),
            pltpu.VMEM((n1 // 2, size), f32),
            pltpu.VMEM((n // 2 - 1, n1 // n, size), f32),
            pltpu.VMEM((n1, size), f32),
            pltpu.VMEM((size, 2 * size), f32),
            pltpu.VMEM((size, size), f32),
            pltpu.VMEM((ydev // 2, size, 2 * stride), f32),
            pltpu.VMEM((size // n // 2, n2, size), f32),
            pltpu.VMEM((size // n // 2, n2, size), f32),
            pltpu.VMEM((n2, size), f32),
            pltpu.VMEM((n2 // 2, size), f32),
            pltpu.VMEM((n // 2 - 1, n2 // n, size), f32),
            pltpu.VMEM((n2, size), f32),
            pltpu.SemaphoreType.DMA((9,)),
            pltpu.SemaphoreType.DMA((9,)),
        ],
        compiler_params=pltpu.CompilerParams(
            collective_id=0, has_side_effects=True, vmem_limit_bytes=32 * 1024 * 1024
        ),
        cost_estimate=pl.CostEstimate(
            flops=600_000_000, bytes_accessed=2_000_000, transcendentals=256
        ),
    )(field, sketch_one, sketch_two, ranks)


def solution(mesh):
    n = mesh.shape["wide"]

    def per_device(field, sketch_one, sketch_two, ranks):
        ydev, kdim, n1 = field.shape
        n2, size = sketch_two.shape
        fits = (
            mesh.shape["narrow"] == 1
            and size == 128
            and n % 2 == 0
            and n >= 4
            and ydev == 8
            and kdim <= size // 2
            and size % (2 * n) == 0
            and n1 % (8 * n) == 0
            and n2 == 8 * n
        )
        if fits:
            return fused(n, field, sketch_one, sketch_two, ranks)
        return general(field, sketch_one, sketch_two, ranks)

    return jax.shard_map(
        per_device,
        mesh=mesh,
        in_specs=(P("wide", "narrow", None), P(), P(), P()),
        out_specs=P("wide", "narrow", None),
        check_vma=False,
    )
```

```python
import functools

import jax
import jax.numpy as jnp
from jax import lax
from jax.experimental import pallas as pl
from jax.experimental.pallas import tpu as pltpu
from jax.sharding import PartitionSpec as P

HIGHEST = lax.Precision.HIGHEST
MESH = pl.DeviceIdType.MESH


def make_basis(local, sketch, rank):
    keep = (jnp.arange(sketch.shape[1]) < rank).astype(jnp.float32)
    masked = sketch * keep
    part = jnp.einsum("akn,ns->aks", local, masked, precision=HIGHEST)
    part = jnp.einsum("akn,aks->ns", local, part, precision=HIGHEST)
    sketched = lax.psum(part, ("wide", "narrow"))
    inner = jnp.dot(sketched.T, sketched, precision=HIGHEST) + jnp.diag(1.0 - keep)
    lower = jnp.linalg.cholesky(inner)
    return jax.scipy.linalg.solve_triangular(lower, sketched.T, lower=True)


def general(field, sketch_one, sketch_two, ranks):
    basis_one = make_basis(field, sketch_one, ranks[0])
    core_one = jnp.einsum("rn,ykn->rky", basis_one, field, precision=HIGHEST)
    regrouped = lax.all_to_all(core_one, "wide", split_axis=0, concat_axis=2, tiled=True)
    basis_two = make_basis(regrouped, sketch_two, ranks[1])
    return jnp.einsum("sn,rkn->rks", basis_two, regrouped, precision=HIGHEST)


def dot(a, b, dims):
    return lax.dot_general(
        a, b, (dims, ((), ())), precision=HIGHEST, preferred_element_type=jnp.float32
    )


NN = ((1,), (0,))
NT = ((1,), (1,))
TN = ((0,), (0,))
BLOCK = 8
TILES = 4


def inverse_factor(work, linv):
    size = linv.shape[0]
    tile = (BLOCK, size)
    group = TILES * BLOCK
    sub = lax.broadcasted_iota(jnp.int32, tile, 0)

    for r0 in range(0, size, group):
        own = work[r0 : r0 + group, :size]
        rest = work[r0 : r0 + group, size:]
        rows_a = [own[u * BLOCK : (u + 1) * BLOCK, :] for u in range(TILES)]
        rows_t = [rest[u * BLOCK : (u + 1) * BLOCK, :] for u in range(TILES)]
        panels_a, panels_t = [], []
        for u in range(TILES):
            d, below = {}, {}
            for q in range(BLOCK):
                lane = r0 + u * BLOCK + q
                column = jnp.broadcast_to(rows_a[u][:, lane : lane + 1], tile)
                for p in range(q, BLOCK):
                    d[p, q] = jnp.broadcast_to(column[p : p + 1, :], tile)
                for v in range(u + 1, TILES):
                    below[v, q] = jnp.broadcast_to(rows_a[v][:, lane : lane + 1], tile)
            done_a, done_t = [], []
            panel_a = jnp.zeros(tile, jnp.float32)
            panel_t = jnp.zeros(tile, jnp.float32)
            for j in range(BLOCK):
                x = d[j, j]
                y = lax.rsqrt(x)
                y = y * (1.5 - 0.5 * ((x * y) * y))
                for p in range(j + 1, BLOCK):
                    d[p, j] = d[p, j] * y
                for v in range(u + 1, TILES):
                    below[v, j] = below[v, j] * y
                for q in range(j + 1, BLOCK):
                    for p in range(q, BLOCK):
                        d[p, q] = d[p, q] - d[p, j] * d[q, j]
                    for v in range(u + 1, TILES):
                        below[v, q] = below[v, q] - below[v, j] * d[q, j]
                ra = jnp.broadcast_to(rows_a[u][j : j + 1, :], tile)
                rt = jnp.broadcast_to(rows_t[u][j : j + 1, :], tile)
                for k in range(j):
                    ra = ra - d[j, k] * done_a[k]
                    rt = rt - d[j, k] * done_t[k]
                ra = ra * y
                rt = rt * y
                done_a.append(ra)
                done_t.append(rt)
                panel_a = jnp.where(sub == j, ra, panel_a)
                panel_t = jnp.where(sub == j, rt, panel_t)
                for v in range(u + 1, TILES):
                    rows_a[v] = rows_a[v] - below[v, j] * ra
                    rows_t[v] = rows_t[v] - below[v, j] * rt
            panels_a.append(panel_a)
            panels_t.append(panel_t)
        panel_t = jnp.concatenate(panels_t, axis=0)
        panel_a = jnp.concatenate(panels_a, axis=0)
        linv[r0 : r0 + group, :] = panel_t
        end = r0 + group
        if end < size:
            both = jnp.concatenate([panel_a, panel_t], axis=1)
            work[end:, :] = work[end:, :] - dot(panel_a.T[end:, :], both, NN)


def fill_work(work, inner, keep_row, size):
    row = lax.broadcasted_iota(jnp.int32, (size, size), 0)
    col = lax.broadcasted_iota(jnp.int32, (size, size), 1)
    eye = (row == col).astype(jnp.float32)
    work[:, :size] = inner + eye * (1.0 - keep_row)
    work[:, size:] = eye


def kernel(
    n, field, sketch_one, sketch_two, ranks, out,
    flat, part_one, pair_one, got_one, full_one, work, linv, core, give, have,
    part_two, got_two, full_two, send_sem, recv_sem,
):
    me = lax.axis_index("wide")
    ydev, kdim, n1 = field.shape
    size = sketch_one.shape[1]
    n2 = sketch_two.shape[0]
    stride = flat.shape[0] // ydev
    per = size // n

    barrier = pltpu.get_barrier_semaphore()

    def greet(i, carry):
        peer = lax.rem(me + 1 + i, n)
        pl.semaphore_signal(barrier, inc=1, device_id={"wide": peer}, device_id_type=MESH)
        return carry

    lax.fori_loop(0, n - 1, greet, 0)

    core_id = lax.rem(me, 2)
    chip = me // 2
    chips = n // 2

    def every(i):
        return lax.rem(me + 1 + i, n)

    def alike(i):
        return 2 * lax.rem(chip + 1 + i, chips) + core_id

    def twin(i):
        return chip * 2 + 1 - core_id

    def exchange(phase, count, peer_of, source, target, whole):
        def start(i, carry):
            peer = peer_of(i)
            pltpu.make_async_remote_copy(
                src_ref=source(peer), dst_ref=target(i),
                send_sem=send_sem.at[phase], recv_sem=recv_sem.at[phase],
                device_id={"wide": peer}, device_id_type=MESH,
            ).start()
            return carry

        lax.fori_loop(0, count, start, 0)
        everything = pltpu.make_async_remote_copy(
            src_ref=whole, dst_ref=whole,
            send_sem=send_sem.at[phase], recv_sem=recv_sem.at[phase],
            device_id={"wide": peer_of(0)}, device_id_type=MESH,
        )
        everything.wait_recv()
        everything.wait_send()

    def sum_over_devices(phase, part, pair, got, full, direct):
        rows = part.shape[0]
        half = rows // 2
        chunk = rows // n

        def half_of(device):
            return pl.ds(pl.multiple_of(lax.rem(device, 2) * half, 8), half)

        def chunk_of(device):
            start = lax.rem(device, 2) * half + (device // 2) * chunk
            return pl.ds(pl.multiple_of(start, 8), chunk)

        mine = half_of(me)
        if direct:
            exchange(
                phase, n - 1, every,
                lambda p: part.at[chunk_of(p), :], lambda i: got.at[i], got,
            )
        else:
            exchange(phase, 1, twin, lambda p: part.at[half_of(p), :], lambda i: pair, pair)
            part[mine, :] = part[mine, :] + pair[...]
            exchange(
                phase + 1, chips - 1, alike,
                lambda p: part.at[chunk_of(p), :], lambda i: got.at[i], got,
            )
        own = chunk_of(me)
        full[own, :] = jnp.sum(got[...], axis=0) + part[own, :]
        if direct:
            exchange(
                phase + 2, n - 1, every,
                lambda p: full.at[own, :], lambda i: full.at[own, :],
                full.at[pl.ds(0, rows - chunk), :],
            )
            return
        exchange(
            phase + 2, chips - 1, alike,
            lambda p: full.at[own, :], lambda i: full.at[own, :],
            full.at[pl.ds(0, half - chunk), :],
        )
        exchange(
            phase + 3, 1, twin,
            lambda p: full.at[mine, :], lambda i: full.at[mine, :],
            full.at[pl.ds(0, half), :],
        )

    lane = lax.broadcasted_iota(jnp.int32, (1, size), 1)
    keep_one = (lane < ranks[0]).astype(jnp.float32)
    keep_two = (lane < ranks[1]).astype(jnp.float32)

    for y in range(ydev):
        flat[y * stride : y * stride + kdim, :] = field[y]
        flat[y * stride + kdim : (y + 1) * stride, :] = jnp.zeros(
            (stride - kdim, n1), jnp.float32
        )
    projected = dot(flat[...], sketch_one[...] * keep_one, NN)
    part_one[...] = dot(projected, flat[...], TN).T
    masked_two = (sketch_two[...] * keep_two).T

    pl.semaphore_wait(barrier, n - 1)

    sum_over_devices(0, part_one, pair_one, got_one, full_one, False)
    sk = full_one[...]
    fill_work(work, dot(sk, sk, TN), keep_one, size)
    rotated = dot(flat[...], sk, NN)
    inverse_factor(work, linv)
    mixed = dot(linv[...], rotated, NT)
    for t in range(ydev // 2):
        core[t] = mixed[:, 2 * stride * t : 2 * stride * (t + 1)]

    low = lax.broadcasted_iota(jnp.int32, (n, 2 * stride), 1) < stride
    for half in range(per // 2):
        for t in range(ydev // 2):
            first = core[t, pl.ds(2 * half, n, stride=per), :]
            second = core[t, pl.ds(2 * half + 1, n, stride=per), :]
            even = jnp.where(low, first, pltpu.roll(second, stride, 1))
            odd = jnp.where(low, pltpu.roll(first, stride, 1), second)
            give[half, pl.ds(2 * t, n, stride=ydev), :] = even
            give[half, pl.ds(2 * t + 1, n, stride=ydev), :] = odd
    mine_y = pl.ds(pl.multiple_of(me * ydev, ydev), ydev)
    have[:, mine_y, :] = give[:, mine_y, :]
    exchange(
        8, n - 1, every,
        lambda p: give.at[:, pl.ds(pl.multiple_of(p * ydev, ydev), ydev), :],
        lambda i: have.at[:, mine_y, :],
        have.at[:, pl.ds(0, n2 - ydev), :],
    )

    total = jnp.zeros((n2, size), jnp.float32)
    for half in range(per // 2):
        fibers = have[half]
        total = total + dot(fibers, dot(masked_two, fibers, NN), NT)
    part_two[...] = total
    sum_over_devices(4, part_two, None, got_two, full_two, True)
    sk = full_two[...]
    fill_work(work, dot(sk, sk, TN), keep_two, size)
    spun = [dot(have[half], sk, TN) for half in range(per // 2)]
    inverse_factor(work, linv)
    for half in range(per // 2):
        done = dot(spun[half], linv[...], NT)
        for i in range(2):
            out[2 * half + i] = done[stride * i : stride * i + kdim, :]


def fused(n, field, sketch_one, sketch_two, ranks):
    ydev, kdim, n1 = field.shape
    n2, size = sketch_two.shape
    stride = size // 2
    vmem = pl.BlockSpec(memory_space=pltpu.VMEM)
    f32 = jnp.float32
    return pl.pallas_call(
        functools.partial(kernel, n),
        out_shape=jax.ShapeDtypeStruct((size // n, kdim, size), f32),
        in_specs=[vmem, vmem, vmem, pl.BlockSpec(memory_space=pltpu.SMEM)],
        out_specs=vmem,
        scratch_shapes=[
            pltpu.VMEM((ydev * stride, n1), f32),
            pltpu.VMEM((n1, size), f32),
            pltpu.VMEM((n1 // 2, size), f32),
            pltpu.VMEM((n // 2 - 1, n1 // n, size), f32),
            pltpu.VMEM((n1, size), f32),
            pltpu.VMEM((size, 2 * size), f32),
            pltpu.VMEM((size, size), f32),
            pltpu.VMEM((ydev // 2, size, 2 * stride), f32),
            pltpu.VMEM((size // n // 2, n2, size), f32),
            pltpu.VMEM((size // n // 2, n2, size), f32),
            pltpu.VMEM((n2, size), f32),
            pltpu.VMEM((n - 1, n2 // n, size), f32),
            pltpu.VMEM((n2, size), f32),
            pltpu.SemaphoreType.DMA((9,)),
            pltpu.SemaphoreType.DMA((9,)),
        ],
        compiler_params=pltpu.CompilerParams(
            collective_id=0, has_side_effects=True, vmem_limit_bytes=32 * 1024 * 1024
        ),
        cost_estimate=pl.CostEstimate(
            flops=600_000_000, bytes_accessed=2_000_000, transcendentals=256
        ),
    )(field, sketch_one, sketch_two, ranks)


def solution(mesh):
    n = mesh.shape["wide"]

    def per_device(field, sketch_one, sketch_two, ranks):
        ydev, kdim, n1 = field.shape
        n2, size = sketch_two.shape
        fits = (
            mesh.shape["narrow"] == 1
            and size == 128
            and n % 2 == 0
            and n >= 4
            and ydev == 8
            and kdim <= size // 2
            and size % (2 * n) == 0
            and n1 % (8 * n) == 0
            and n2 == 8 * n
        )
        if fits:
            return fused(n, field, sketch_one, sketch_two, ranks)
        return general(field, sketch_one, sketch_two, ranks)

    return jax.shard_map(
        per_device,
        mesh=mesh,
        in_specs=(P("wide", "narrow", None), P(), P(), P()),
        out_specs=P("wide", "narrow", None),
        check_vma=False,
    )
```
